256 devices in a mesh: ep: 8 (over x, core), et: 32 (over z, y).
Axes of the slice: x: 4, y: 4, z: 8, core: 2. Of those that a mesh axis runs over, the one named last changes fastest.
Arguments:
- d_out: bfloat16 [2048, 3072], P('ep', 'et'), may hold values from -6 to 6
- gate_weights: bfloat16 [2048, 2], P('ep'), may hold values from 0.19921875 to 1
- expert_ids: int32 [2048, 2], P('ep'), may hold values from 0 to 7, all different within a row; in each aligned block of 256 rows (0 to 255, 256 to 511, ...) at most 128 rows name the same one
- saved_inputs: bfloat16 [8192, 3072], P('ep', 'et'), may hold values from -6 to 6
- w_gate: bfloat16 [8, 3072, 8192], P('ep', None, 'et'), may hold values from -0.109375 to 0.109375
- w_up: bfloat16 [8, 3072, 8192], P('ep', None, 'et'), may hold values from -0.109375 to 0.109375
- w_down: bfloat16 [8, 8192, 3072], P('ep', 'et'), may hold values from -0.0625 to 0.0625
Outputs:
- d_tokens: bfloat16 [2048, 3072], P('ep', 'et')
- d_gates: float32 [2048, 2], P('ep')
- d_w_gate: bfloat16 [8, 3072, 8192], P('ep', None, 'et')
- d_w_up: bfloat16 [8, 3072, 8192], P('ep', None, 'et')
- d_w_down: bfloat16 [8, 8192, 3072], P('ep', 'et')
The draws below stay inside these ranges and needn't reach their ends.
Inputs may be any that keep to these rules, and one draw needn't show every extreme that they name: `expert_ids`: each row names two different experts. Within the rows of one index of ep (aligned blocks of 256 rows) no expert is named more than 128 times, a bound that some block reaches.
All inputs are finite; a program needn't handle non-finite values.
Results may differ from the reference program's by a relative error of at most 0.011.
Values may be sent and summed in bfloat16 or wider, within the bound.
No kernel may reach another device: no remote copies, remote signals or barrier semaphores. Data moves between devices by JAX's collectives and lax.ppermute only.
A program may use at most 128 MiB of HBM per device.

```python
import math
import jax
import jax.numpy as jnp
import numpy as np
from jax import lax

D = 3072
FF = 8192
TOK_EP = 256
TOP = 2
EXPERTS = 8
MOST = 128
TOKENS = 2048
SLOTS = 8192


def steps_of(stream_key, extent, split, low, top_value):
    def one(dim, blocks):
        heights = jax.random.uniform(jax.random.fold_in(jax.random.fold_in(stream_key, 6), dim), (blocks,), jnp.float32, low / len(split), top_value / len(split))
        return jnp.repeat(jnp.exp(heights), extent[dim] // blocks).reshape((-1,) + (1,) * (len(extent) - dim - 1))

    factor_of = one(*split[0])
    for cut in split[1:]:
        factor_of = factor_of * one(*cut)
    return factor_of


def shared_out(rng, own, number, rows, number_of, top, bound, slope):
    ranking = jax.random.permutation(rng, number_of)
    heavy_load, common = shares(number_of, rows * top, bound, slope, True), shares(number_of, rows * top, bound, slope, False)
    places = jnp.arange(number_of)

    def named(sizes, offset_by):
        used = int((sizes > 0).sum())
        fixed = max(1, used // 4)
        passed = fixed + (places - fixed + offset_by * (used - fixed)) % max(1, number_of - fixed)
        return jnp.zeros((number_of,), jnp.int32).at[ranking[jnp.where(places < fixed, places, passed)]].set(jnp.asarray(sizes, jnp.int32))

    sizes = jnp.where(number % 4 == 0, named(heavy_load, number // 4), named(common, number - number // 4 - 1))
    mixed = jax.random.permutation(jax.random.fold_in(own, 3), number_of)
    giver, taker = mixed[0:number_of // 2 * 2:2], mixed[1:number_of // 2 * 2:2]
    margin = jnp.minimum(sizes[giver] - 1, bound - sizes[taker]) // 2
    margin = jnp.where((giver == ranking[0]) | (taker == ranking[0]) | (sizes[taker] == 0), 0, jnp.maximum(margin, 0))
    passed = jax.random.randint(jax.random.fold_in(own, 4), (number_of // 2,), 0, 1 << 20) % (margin + 1)
    sizes = sizes.at[giver].add(-passed).at[taker].add(passed)
    items = jnp.searchsorted(jnp.cumsum(sizes), jnp.arange(rows * top), side="right").astype(jnp.int32)
    table = items.reshape(top, rows).T
    table = table[jax.random.permutation(jax.random.fold_in(own, 1), rows)]
    offset_by = jax.random.randint(jax.random.fold_in(own, 2), (rows, 1), 0, top)
    return jnp.take_along_axis(table, (jnp.arange(top)[None, :] + offset_by) % top, axis=1)


def shares(amount, total, most, lean, full):
    loads = [(1 << 20) // math.isqrt(grade ** lean) + 1 for grade in range(1, amount + 1)]
    largest = most if full else min(most, max(-(-total // amount), total * loads[0] // sum(loads)))
    least = 1 if total - largest >= amount - 1 else 0
    holding, rest = [largest] + [least] * (amount - 1), total - largest - least * (amount - 1)
    while rest > 0:
        movable = [i for i in range(1, amount) if holding[i] < largest] or [i for i in range(1, amount) if holding[i] < most]
        mass, remaining = sum([loads[i] for i in movable]), rest
        for i in movable:
            more = min(most - holding[i], max(1, remaining * loads[i] // mass), rest)
            holding[i] = holding[i] + more
            rest = rest - more
    return np.array(holding)


def scatter_about(key, shape, deviation, bound, split=(), kind=jnp.bfloat16):
    drawn = deviation * jax.random.normal(key, shape, jnp.float32)
    if split:
        drawn = drawn * steps_of(key, shape, split, -0.22, 0.18)
    return jnp.clip(drawn, -bound, bound).astype(kind)


def setup_inputs(seed: int = 0) -> dict:
    arg_keys = jax.random.split(jax.random.key(seed), 8)
    d_out = scatter_about(arg_keys[0], (TOKENS, D), 1.0, 6.0, ((0, 8), (1, 32)))
    gate_weights = jnp.clip(0.19921875 + 0.80078125 * jax.random.uniform(arg_keys[1], (TOKENS, TOP), jnp.float32) ** steps_of(arg_keys[1], (TOKENS, TOP), ((0, 8),), -0.2, 0.2), 0.19921875, 1.0).astype(jnp.bfloat16)
    expert_ids_keys = jax.random.split(jax.random.fold_in(arg_keys[2], 1), TOKENS // TOK_EP)
    expert_ids_turns = jax.random.permutation(jax.random.fold_in(arg_keys[2], 3), TOKENS // TOK_EP)
    expert_ids = jax.vmap(lambda own, number: shared_out(jax.random.fold_in(arg_keys[2], 2), own, number, TOK_EP, EXPERTS, 2, MOST, 2))(expert_ids_keys, expert_ids_turns).reshape((TOKENS, TOP))
    saved_inputs = scatter_about(arg_keys[3], (SLOTS, D), 1.0, 6.0, ((0, 8), (1, 32)))
    w_gate = scatter_about(arg_keys[4], (EXPERTS, D, FF), D ** -0.5, 0.109375, ((0, 8), (2, 32)))
    w_up = scatter_about(arg_keys[5], (EXPERTS, D, FF), D ** -0.5, 0.109375, ((0, 8), (2, 32)))
    w_down = scatter_about(arg_keys[6], (EXPERTS, FF, D), FF ** -0.5, 0.0625, ((0, 8), (1, 32)))
    return dict(d_out=d_out, gate_weights=gate_weights, expert_ids=expert_ids, saved_inputs=saved_inputs, w_gate=w_gate, w_up=w_up, w_down=w_down)


def slot_places(expert_ids):
    tokens = expert_ids.shape[0]
    experts = EXPERTS
    flat = expert_ids.reshape(-1)
    onehot = (flat[:, None] == jnp.arange(experts, dtype=jnp.int32)[None, :]).astype(jnp.int32)
    blocks = onehot.reshape(tokens // TOK_EP, 2 * TOK_EP, experts)
    before = jnp.cumsum(blocks, axis=1) - blocks
    slot = jnp.sum(before * blocks, axis=2).reshape(-1).astype(jnp.int32)
    source = (jnp.arange(2 * tokens, dtype=jnp.int32) // (2 * TOK_EP)).astype(jnp.int32)
    return ((flat * experts + source) * MOST + slot).astype(jnp.int32)


def expert_pass(inputs, routed, gates, wg, wu, wd):
    gate_pre = jnp.dot(inputs, wg, preferred_element_type=jnp.float32)
    up_pre = jnp.dot(inputs, wu, preferred_element_type=jnp.float32)
    sig = jax.nn.sigmoid(gate_pre)
    act = gate_pre * sig
    hidden = (act * up_pre).astype(jnp.bfloat16)
    grad_hidden = jnp.dot(routed, wd.T, preferred_element_type=jnp.float32)
    slot_gate = jnp.sum(hidden.astype(jnp.float32) * grad_hidden, axis=1)
    gates_col = gates[:, None]
    weighted = (gates_col * routed).astype(jnp.bfloat16)
    d_w_down = jnp.dot(hidden.T, weighted, preferred_element_type=jnp.float32).astype(jnp.bfloat16)
    d_act = gates_col.astype(jnp.float32) * grad_hidden
    grad_gate = (d_act * up_pre * sig * (1.0 + gate_pre * (1.0 - sig))).astype(jnp.bfloat16)
    grad_up = (d_act * act).astype(jnp.bfloat16)
    d_w_gate = jnp.dot(inputs.T, grad_gate, preferred_element_type=jnp.float32).astype(jnp.bfloat16)
    d_w_up = jnp.dot(inputs.T, grad_up, preferred_element_type=jnp.float32).astype(jnp.bfloat16)
    slot_input = jnp.dot(grad_gate, wg.T, preferred_element_type=jnp.float32) + jnp.dot(grad_up, wu.T, preferred_element_type=jnp.float32)
    return slot_gate, slot_input, d_w_gate, d_w_up, d_w_down


def reference(d_out, gate_weights, expert_ids, saved_inputs, w_gate, w_up, w_down):
    tokens = expert_ids.shape[0]
    experts = EXPERTS
    width = d_out.shape[1]
    place = slot_places(expert_ids)
    rows = experts * experts * MOST
    repeated = jnp.repeat(d_out, 2, axis=0)
    routed = jnp.zeros((rows, width), d_out.dtype).at[place].set(repeated)
    routed_gates = jnp.zeros((rows,), gate_weights.dtype).at[place].set(gate_weights.reshape(-1))
    per_rows = experts * MOST

    def one_expert(items):
        return expert_pass(*items)

    slot_gate, slot_input, d_w_gate, d_w_up, d_w_down = lax.map(one_expert, (
        saved_inputs.reshape(experts, per_rows, width),
        routed.reshape(experts, per_rows, width),
        routed_gates.reshape(experts, per_rows),
        w_gate, w_up, w_down))
    picked = slot_input.reshape(rows, width)[place].reshape(tokens, 2, width)
    d_tokens = (picked[:, 0, :] + picked[:, 1, :]).astype(jnp.bfloat16)
    d_gates = slot_gate.reshape(-1)[place].reshape(tokens, 2)
    return d_tokens, d_gates, d_w_gate, d_w_up, d_w_down
```

```python
import jax
import jax.numpy as jnp
from jax import lax
from jax.sharding import Mesh, PartitionSpec as P

BF = jnp.bfloat16
F32 = jnp.float32


def dot(left, right, dims, out=F32):
    return lax.dot_general(left, right, (dims, ((), ())), preferred_element_type=out)


def move(v, axis, step):
    n = lax.axis_size(axis)
    return lax.ppermute(v, axis, [(i, (i + step) % n) for i in range(n)])


def swap(v, axis, mask):
    n = lax.axis_size(axis)
    return lax.ppermute(v, axis, [(i, i ^ mask) for i in range(n)])


def at(v, index, dim):
    return lax.dynamic_index_in_dim(v, index, dim, keepdims=False)


def put(buf, v, index, dim):
    return lax.dynamic_update_index_in_dim(buf, v, index, dim)


def ring_gather(v, axis, place, split):
    n = lax.axis_size(axis)
    me = lax.axis_index(axis)
    far = n // 2
    place(v, me, None)
    right = left = v
    for k in range(1, far):
        right = move(right, axis, 1)
        left = move(left, axis, -1)
        place(right, (me - k) % n, None)
        place(left, (me + k) % n, None)
    if split:
        half = v.shape[0] // 2
        place(move(right[:half], axis, 1), (me + far) % n, 0)
        place(move(left[half:], axis, -1), (me + far) % n, 1)
    else:
        place(move(right, axis, 1), (me + far) % n, None)


def gather_two_axes(x):
    rows, n = x.shape
    nz, ny = lax.axis_size("z"), lax.axis_size("y")
    h = rows // 2
    full = [jnp.zeros((nz, ny, 2, h, n), x.dtype)]

    def first(v, axis):
        size = lax.axis_size(axis)
        buf = [jnp.zeros((size, h, n), x.dtype)]

        def place(piece, owner, part):
            buf[0] = put(buf[0], piece, owner, 0)

        ring_gather(v, axis, place, False)
        return buf[0]

    def place_a(piece, owner, part):
        start = (0 if part in (None, 0) else nz // 2, owner, 0, 0, 0)
        full[0] = lax.dynamic_update_slice(full[0], piece[:, None, None], start)

    def place_b(piece, owner, part):
        start = (owner, 0 if part in (None, 0) else ny // 2, 1, 0, 0)
        full[0] = lax.dynamic_update_slice(full[0], piece[None, :, None], start)

    part_a = first(x[:h], "z")
    part_b = first(x[h:], "y")
    ring_gather(part_b, "z", place_b, True)
    ring_gather(part_a, "y", place_a, True)
    return full[0].reshape(nz * ny * rows, n)


def ring_scatter(take, axis, split):
    n = lax.axis_size(axis)
    me = lax.axis_index(axis)
    far = n // 2
    right, left = None, None
    term = take((me + far) % n)
    if split:
        half = term.shape[0] // 2
        right = move(term[:half].astype(BF), axis, 1)
        left = move(term[half:].astype(BF), axis, -1)
        pad = jnp.zeros((half,) + term.shape[1:], F32)
        right = jnp.concatenate([right.astype(F32), pad], 0)
        left = jnp.concatenate([pad, left.astype(F32)], 0)
    else:
        right = move(term.astype(BF), axis, 1).astype(F32)
    for k in range(far - 1, 0, -1):
        right = move((take((me + k) % n) + right).astype(BF), axis, 1).astype(F32)
        out = take((me - k) % n)
        out = out if left is None else out + left
        left = move(out.astype(BF), axis, -1).astype(F32)
    return take(me) + right + left


def scatter_two_axes(s):
    nz, ny = lax.axis_size("z"), lax.axis_size("y")
    n = s.shape[1]
    h = s.shape[0] // (nz * ny * 2)
    s = s.reshape(nz, ny, 2, h, n)
    sum_a = ring_scatter(lambda y: at(s[:, :, 0], y, 1).astype(F32), "y", True)
    sum_b = ring_scatter(lambda z: at(s[:, :, 1], z, 0).astype(F32), "z", True)
    sum_a = ring_scatter(lambda z: at(sum_a, z, 0), "z", False)
    sum_b = ring_scatter(lambda y: at(sum_b, y, 0), "y", False)
    return jnp.concatenate([sum_a, sum_b], 0)


def tree(terms):
    while len(terms) > 1:
        terms = [terms[i] + terms[i + 1] for i in range(0, len(terms), 2)]
    return terms[0]


def sum_all(v):
    for axis in ("z", "y"):
        n = lax.axis_size(axis)
        v = tree([v] + [swap(v, axis, m) for m in range(1, n)])
    return v


def shards(d_out, gate_weights, expert_ids, saved_inputs, w_gate, w_up, w_down):
    experts = lax.axis_size("x") * lax.axis_size("c")
    tok_rows, feats = d_out.shape
    most = tok_rows // 2
    slots = experts * most
    weight_gate, weight_up, weight_down = w_gate[0], w_up[0], w_down[0]

    flat = expert_ids.reshape(-1)
    onehot = (flat[:, None] == jnp.arange(experts, dtype=jnp.int32)[None, :]).astype(jnp.int32)
    before = jnp.cumsum(onehot, axis=0) - onehot
    place = (flat * most + jnp.sum(before * onehot, axis=1)).reshape(tok_rows, 2)
    lanes = jnp.arange(slots, dtype=jnp.int32)[None, :]
    hit0 = place[:, 0:1] == lanes
    hit1 = place[:, 1:2] == lanes
    chosen = (hit0 | hit1).astype(BF)
    zero = jnp.zeros((), F32)
    gates_out = jnp.sum(
        jnp.where(hit0, gate_weights[:, 0:1].astype(F32), zero)
        + jnp.where(hit1, gate_weights[:, 1:2].astype(F32), zero),
        axis=0,
    ).astype(BF)
    outgoing = dot(d_out, chosen, ((0,), (0,)), BF)
    extra = jnp.concatenate([gates_out[None], jnp.zeros((15, slots), BF)], 0)
    outgoing = jnp.concatenate([outgoing, extra], 0).reshape(feats + 16, experts, most)
    arrived = lax.all_to_all(
        outgoing.transpose(1, 0, 2), ("x", "c"), split_axis=0, concat_axis=0, tiled=True
    )
    arrived = arrived.transpose(1, 0, 2).reshape(feats + 16, slots)
    gates = arrived[feats : feats + 1].astype(F32)

    inputs = gather_two_axes(saved_inputs.T)
    routed = gather_two_axes(arrived[:feats])

    gate_pre = dot(weight_gate, inputs, ((0,), (0,)))
    up_pre = dot(weight_up, inputs, ((0,), (0,)))
    sig = jax.nn.sigmoid(gate_pre)
    act = gate_pre * sig
    hidden = (act * up_pre).astype(BF)
    hidden_gated = (hidden.astype(F32) * gates).astype(BF)
    slope = up_pre * sig * (1.0 + gate_pre * (1.0 - sig))
    grad_hidden = dot(weight_down, routed, ((1,), (0,)))
    partial_gate = jnp.sum(hidden.astype(F32) * grad_hidden, axis=0, keepdims=True)
    d_act = gates * grad_hidden
    grad_gate = (d_act * slope).astype(BF)
    grad_up = (d_act * act).astype(BF)
    partial = (
        dot(weight_gate, grad_gate, ((1,), (0,))) + dot(weight_up, grad_up, ((1,), (0,)))
    ).astype(BF)
    share = scatter_two_axes(partial)
    slot_gate = sum_all(partial_gate)
    d_w_down = dot(hidden_gated, routed, ((1,), (1,)), BF)
    d_w_gate = dot(inputs, grad_gate, ((1,), (1,)), BF)
    d_w_up = dot(inputs, grad_up, ((1,), (1,)), BF)

    send = jnp.concatenate([share, slot_gate, jnp.zeros((7, slots), F32)], 0)
    send = send.reshape(feats + 8, experts, most).transpose(1, 0, 2)
    back = lax.all_to_all(send, ("x", "c"), split_axis=0, concat_axis=0, tiled=True)
    back = back.transpose(1, 0, 2).reshape(feats + 8, slots)
    share_back = back[:feats]
    high = share_back.astype(BF)
    low = (share_back - high.astype(F32)).astype(BF)
    d_tokens = dot(chosen, high, ((1,), (1,))) + dot(chosen, low, ((1,), (1,)))
    d_tokens = d_tokens.astype(BF)
    gate_back = back[feats : feats + 1]
    d_gates = jnp.stack(
        [jnp.sum(jnp.where(hit, gate_back, zero), axis=1) for hit in (hit0, hit1)], axis=1
    )
    return (d_tokens, d_gates, d_w_gate[None], d_w_up[None], d_w_down[None])


def solution(mesh):
    ep, et = mesh.axis_names
    nep, net = mesh.shape[ep], mesh.shape[et]
    fine = Mesh(mesh.devices.reshape(nep // 2, 2, net // 4, 4), ("x", "c", "z", "y"))
    e, t = ("x", "c"), ("z", "y")
    return jax.shard_map(
        shards,
        mesh=fine,
        in_specs=(P(e, t), P(e, None), P(e, None), P(e, t), P(e, None, t), P(e, None, t), P(e, t, None)),
        out_specs=(P(e, t), P(e, None), P(e, None, t), P(e, None, t), P(e, t, None)),
        check_vma=False,
    )
```

```python
import jax
import jax.numpy as jnp
from jax import lax
from jax.sharding import Mesh, PartitionSpec as P

BF = jnp.bfloat16
F32 = jnp.float32


def dot(left, right, dims, out=F32):
    return lax.dot_general(left, right, (dims, ((), ())), preferred_element_type=out)


def move(v, axis, step):
    n = lax.axis_size(axis)
    return lax.ppermute(v, axis, [(i, (i + step) % n) for i in range(n)])


def at(v, index, dim):
    return lax.dynamic_index_in_dim(v, index, dim, keepdims=False)


def put(buf, v, index, dim):
    return lax.dynamic_update_index_in_dim(buf, v, index, dim)


def ring_gather(v, axis, place, split):
    n = lax.axis_size(axis)
    me = lax.axis_index(axis)
    far = n // 2
    place(v, me, None)
    right = left = v
    for k in range(1, far):
        right = move(right, axis, 1)
        left = move(left, axis, -1)
        place(right, (me - k) % n, None)
        place(left, (me + k) % n, None)
    if split:
        half = v.shape[0] // 2
        place(move(right[:half], axis, 1), (me + far) % n, 0)
        place(move(left[half:], axis, -1), (me + far) % n, 1)
    else:
        place(move(right, axis, 1), (me + far) % n, None)


def gather_two_axes(x, order):
    rows, n = x.shape
    nz, ny = lax.axis_size("z"), lax.axis_size("y")
    size = lax.axis_size(order[0])
    part_of = [jnp.zeros((size, rows, n), x.dtype)]
    full = [jnp.zeros((nz, ny, rows, n), x.dtype)]

    def place_first(piece, owner, part):
        part_of[0] = put(part_of[0], piece, owner, 0)

    def place_second(piece, owner, part):
        low = 0 if part in (None, 0) else size // 2
        if order[0] == "z":
            full[0] = lax.dynamic_update_slice(full[0], piece[:, None], (low, owner, 0, 0))
        else:
            full[0] = lax.dynamic_update_slice(full[0], piece[None], (owner, low, 0, 0))

    ring_gather(x, order[0], place_first, False)
    ring_gather(part_of[0], order[1], place_second, True)
    return full[0].reshape(nz * ny * rows, n)


def ring_scatter(take, axis, split):
    n = lax.axis_size(axis)
    me = lax.axis_index(axis)
    far = n // 2
    left = None
    if split:
        right = move(take((me + far) % n, 0).astype(BF), axis, 1)
        seen = [right]
        right = right.astype(F32)
        left = move(take((me + far) % n, 1).astype(BF), axis, -1).astype(F32)
        pad = jnp.zeros_like(right)
        right = jnp.concatenate([right, pad], 0)
        left = jnp.concatenate([pad, left], 0)
    else:
        right = move(take((me + far) % n, None).astype(BF), axis, 1)
        seen = [right]
        right = right.astype(F32)
    for k in range(far - 1, 0, -1):
        right = move((take((me + k) % n, None) + right).astype(BF), axis, 1)
        seen.append(right)
        right = right.astype(F32)
        out = take((me - k) % n, None)
        out = out if left is None else out + left
        left = move(out.astype(BF), axis, -1).astype(F32)
    return take(me, None) + right + left, seen


def halved(v, part):
    half = v.shape[0] // 2
    return v if part is None else v[:half] if part == 0 else v[half:]


def scatter_two_axes(weights, grads, order):
    nz, ny, rows, k = weights.shape
    n = grads.shape[1]

    def take_first(owner, part):
        own = halved(at(weights, owner, "zy".index(order[0])), part)
        return dot(own.reshape(-1, k), grads, ((1,), (0,))).reshape(-1, rows, n)

    total, seen = ring_scatter(take_first, order[0], True)
    return ring_scatter(lambda owner, part: at(total, owner, 0), order[1], False)[0], seen


def fence(*values):
    return lax.optimization_barrier(values)


def three_parts(v):
    rows = []
    for _ in range(3):
        part = lax.reduce_precision(v, 8, 7)
        rows.append(part.astype(BF))
        v = v - part
    return rows


def sum_all(v):
    size = lax.axis_size("z") * lax.axis_size("y")
    rows = jnp.broadcast_to(v, (size, v.shape[1]))
    rows = lax.all_to_all(rows, ("z", "y"), split_axis=0, concat_axis=0, tiled=True)
    return jnp.sum(rows, axis=0, keepdims=True)


def shards(d_out, gate_weights, expert_ids, saved_inputs, w_gate, w_up, w_down):
    experts = lax.axis_size("x") * lax.axis_size("c")
    tok_rows, feats = d_out.shape
    most = tok_rows // 2
    slots = experts * most
    weight_gate, weight_up, weight_down = w_gate[0], w_up[0], w_down[0]

    flat = expert_ids.reshape(-1)
    onehot = (flat[:, None] == jnp.arange(experts, dtype=jnp.int32)[None, :]).astype(jnp.int32)
    before = jnp.cumsum(onehot, axis=0) - onehot
    place = (flat * most + jnp.sum(before * onehot, axis=1)).reshape(tok_rows, 2)
    lanes = jnp.arange(slots, dtype=jnp.int32)[None, :]
    hit0 = place[:, 0:1] == lanes
    hit1 = place[:, 1:2] == lanes
    chosen = (hit0 | hit1).astype(BF)
    zero = jnp.zeros((), F32)
    gates_out = jnp.sum(
        jnp.where(hit0, gate_weights[:, 0:1].astype(F32), zero)
        + jnp.where(hit1, gate_weights[:, 1:2].astype(F32), zero),
        axis=0,
    ).astype(BF)
    outgoing = dot(d_out, chosen, ((0,), (0,)), BF)
    extra = jnp.concatenate([gates_out[None], jnp.zeros((15, slots), BF)], 0)
    outgoing = jnp.concatenate([outgoing, extra], 0).reshape(feats + 16, experts, most)
    arrived = lax.all_to_all(
        outgoing.transpose(1, 0, 2), ("x", "c"), split_axis=0, concat_axis=0, tiled=True
    )
    arrived = arrived.transpose(1, 0, 2).reshape(feats + 16, slots)
    gates = arrived[feats : feats + 1].astype(F32)

    inputs = gather_two_axes(saved_inputs.T, "zy")
    routed = gather_two_axes(arrived[:feats], "yz")

    both = jnp.concatenate([weight_gate, weight_up], 1)
    both = both.reshape(lax.axis_size("z"), lax.axis_size("y"), feats, -1)
    gate_pre = dot(weight_gate, inputs, ((0,), (0,)))
    up_pre = dot(weight_up, inputs, ((0,), (0,)))
    sig = jax.nn.sigmoid(gate_pre)
    act = gate_pre * sig
    hidden = (act * up_pre).astype(BF)
    hidden_gated = (hidden.astype(F32) * gates).astype(BF)
    slope = up_pre * sig * (1.0 + gate_pre * (1.0 - sig))
    grad_hidden = dot(weight_down, routed, ((1,), (0,)))
    partial_gate = jnp.sum(hidden.astype(F32) * grad_hidden, axis=0, keepdims=True)
    d_act = gates * grad_hidden
    grad_gate = (d_act * slope).astype(BF)
    grad_up = (d_act * act).astype(BF)
    grads = jnp.concatenate([grad_gate, grad_up], 0)
    half = slots // 2
    share_a, _ = scatter_two_axes(both, grads[:, :half], "yz")
    share_b, seen = scatter_two_axes(both, grads[:, half:], "zy")
    share = jnp.concatenate([share_a, share_b], 1).astype(BF)
    slot_gate = sum_all(partial_gate)
    d_w_down = dot(fence(hidden_gated, seen[1])[0], routed, ((1,), (1,)), BF)
    d_w_gate = dot(inputs, fence(grad_gate, seen[2])[0], ((1,), (1,)), BF)
    d_w_up = dot(inputs, fence(grad_up, seen[3])[0], ((1,), (1,)), BF)

    send = jnp.concatenate([share] + three_parts(slot_gate) + [jnp.zeros((13, slots), BF)], 0)
    send = send.reshape(feats + 16, experts, most).transpose(1, 0, 2)
    back = lax.all_to_all(send, ("x", "c"), split_axis=0, concat_axis=0, tiled=True)
    back = back.transpose(1, 0, 2).reshape(feats + 16, slots)
    d_tokens = dot(chosen, back[:feats], ((1,), (1,)), BF)
    gate_back = jnp.sum(back[feats : feats + 3].astype(F32), axis=0)[None]
    lanes = jnp.arange(slots, dtype=jnp.int32)[None, :]
    zero = jnp.zeros((), F32)
    d_gates = jnp.stack(
        [jnp.sum(jnp.where(place[:, k : k + 1] == lanes, gate_back, zero), axis=1) for k in (0, 1)],
        axis=1,
    )
    return (d_tokens, d_gates, d_w_gate[None], d_w_up[None], d_w_down[None])


def solution(mesh):
    ep, et = mesh.axis_names
    nep, net = mesh.shape[ep], mesh.shape[et]
    fine = Mesh(mesh.devices.reshape(nep // 2, 2, net // 4, 4), ("x", "c", "z", "y"))
    e, t = ("x", "c"), ("z", "y")
    return jax.shard_map(
        shards,
        mesh=fine,
        in_specs=(P(e, t), P(e, None), P(e, None), P(e, t), P(e, None, t), P(e, None, t), P(e, t, None)),
        out_specs=(P(e, t), P(e, None), P(e, None, t), P(e, None, t), P(e, t, None)),
        check_vma=False,
    )
```

```python
import jax
import jax.numpy as jnp
from jax import lax
from jax.sharding import Mesh, PartitionSpec as P

BF = jnp.bfloat16
F32 = jnp.float32


def dot(left, right, dims, out=F32):
    return lax.dot_general(left, right, (dims, ((), ())), preferred_element_type=out)


def move(v, axis, step):
    n = lax.axis_size(axis)
    return lax.ppermute(v, axis, [(i, (i + step) % n) for i in range(n)])


def at(v, index, dim):
    return lax.dynamic_index_in_dim(v, index, dim, keepdims=False)


def put(buf, v, index, dim):
    return lax.dynamic_update_index_in_dim(buf, v, index, dim)


def ring_gather(v, axis, place, split):
    n = lax.axis_size(axis)
    me = lax.axis_index(axis)
    far = n // 2
    place(v, me, None)
    right = left = v
    for k in range(1, far):
        right = move(right, axis, 1)
        left = move(left, axis, -1)
        place(right, (me - k) % n, None)
        place(left, (me + k) % n, None)
    if split:
        half = v.shape[0] // 2
        place(move(right[:half], axis, 1), (me + far) % n, 0)
        place(move(left[half:], axis, -1), (me + far) % n, 1)
    else:
        place(move(right, axis, 1), (me + far) % n, None)


def gather_two_axes(x, order):
    rows, n = x.shape
    nz, ny = lax.axis_size("z"), lax.axis_size("y")
    size = lax.axis_size(order[0])
    part_of = [jnp.zeros((size, rows, n), x.dtype)]
    full = [jnp.zeros((nz, ny, rows, n), x.dtype)]

    def place_first(piece, owner, part):
        part_of[0] = put(part_of[0], piece, owner, 0)

    def place_second(piece, owner, part):
        low = 0 if part in (None, 0) else size // 2
        if order[0] == "z":
            full[0] = lax.dynamic_update_slice(full[0], piece[:, None], (low, owner, 0, 0))
        else:
            full[0] = lax.dynamic_update_slice(full[0], piece[None], (owner, low, 0, 0))

    ring_gather(x, order[0], place_first, False)
    ring_gather(part_of[0], order[1], place_second, True)
    return full[0].reshape(nz * ny * rows, n)


def ring_scatter(take, axis, split):
    n = lax.axis_size(axis)
    me = lax.axis_index(axis)
    far = n // 2
    left = None
    wait = None
    if split:
        right = move(take((me + far) % n, 0).astype(BF), axis, 1)
        seen = [right]
        right = right.astype(F32)
        left = move(take((me + far) % n, 1).astype(BF), axis, -1).astype(F32)
        pad = jnp.zeros_like(right)
        right = jnp.concatenate([right, pad], 0)
        left = jnp.concatenate([pad, left], 0)
    else:
        right = move(take((me + far) % n, None).astype(BF), axis, 1)
        seen = [right]
        right = right.astype(F32)
    for k in range(far - 1, 0, -1):
        right = move((take((me + k) % n, None, seen[0]) + right).astype(BF), axis, 1)
        seen.append(right)
        right = right.astype(F32)
        out = take((me - k) % n, None, seen[0])
        out = out if left is None else out + left
        left = move(out.astype(BF), axis, -1).astype(F32)
    return take(me, None, seen[0]) + right + left, seen


def halved(v, part):
    half = v.shape[0] // 2
    return v if part is None else v[:half] if part == 0 else v[half:]


def scatter_two_axes(weights, grads, order):
    nz, ny, rows, k = weights.shape
    n = grads.shape[1]

    def take_first(owner, part, arrived=None):
        after = grads if arrived is None else fence(grads, arrived)[0]
        own = halved(at(weights, owner, "zy".index(order[0])), part)
        return dot(own.reshape(-1, k), after, ((1,), (0,))).reshape(-1, rows, n)

    total, seen = ring_scatter(take_first, order[0], True)
    return ring_scatter(lambda owner, part, arrived=None: at(total, owner, 0), order[1], False)[0], seen


def fence(*values):
    return lax.optimization_barrier(values)


def three_parts(v):
    rows = []
    for _ in range(3):
        part = lax.reduce_precision(v, 8, 7)
        rows.append(part.astype(BF))
        v = v - part
    return rows


def sum_all(v):
    size = lax.axis_size("z") * lax.axis_size("y")
    rows = jnp.broadcast_to(v, (size, v.shape[1]))
    rows = lax.all_to_all(rows, ("z", "y"), split_axis=0, concat_axis=0, tiled=True)
    return jnp.sum(rows, axis=0, keepdims=True)


def shards(d_out, gate_weights, expert_ids, saved_inputs, w_gate, w_up, w_down):
    experts = lax.axis_size("x") * lax.axis_size("c")
    tok_rows, feats = d_out.shape
    most = tok_rows // 2
    slots = experts * most
    weight_gate, weight_up, weight_down = w_gate[0], w_up[0], w_down[0]

    flat = expert_ids.reshape(-1)
    onehot = (flat[:, None] == jnp.arange(experts, dtype=jnp.int32)[None, :]).astype(jnp.int32)
    before = jnp.cumsum(onehot, axis=0) - onehot
    place = (flat * most + jnp.sum(before * onehot, axis=1)).reshape(tok_rows, 2)
    lanes = jnp.arange(slots, dtype=jnp.int32)[None, :]
    hit0 = place[:, 0:1] == lanes
    hit1 = place[:, 1:2] == lanes
    chosen = (hit0 | hit1).astype(BF)
    zero = jnp.zeros((), F32)
    gates_out = jnp.sum(
        jnp.where(hit0, gate_weights[:, 0:1].astype(F32), zero)
        + jnp.where(hit1, gate_weights[:, 1:2].astype(F32), zero),
        axis=0,
    ).astype(BF)
    outgoing = dot(d_out, chosen, ((0,), (0,)), BF)
    extra = jnp.concatenate([gates_out[None], jnp.zeros((15, slots), BF)], 0)
    outgoing = jnp.concatenate([outgoing, extra], 0).reshape(feats + 16, experts, most)
    arrived = lax.all_to_all(
        outgoing.transpose(1, 0, 2), ("x", "c"), split_axis=0, concat_axis=0, tiled=True
    )
    arrived = arrived.transpose(1, 0, 2).reshape(feats + 16, slots)
    gates = arrived[feats : feats + 1].astype(F32)

    inputs = gather_two_axes(saved_inputs.T, "zy")
    routed = gather_two_axes(arrived[:feats], "yz")

    both = jnp.concatenate([weight_gate, weight_up], 1)
    both = both.reshape(lax.axis_size("z"), lax.axis_size("y"), feats, -1)
    gate_pre = dot(weight_gate, inputs, ((0,), (0,)))
    up_pre = dot(weight_up, inputs, ((0,), (0,)))
    sig = jax.nn.sigmoid(gate_pre)
    act = gate_pre * sig
    hidden = (act * up_pre).astype(BF)
    hidden_gated = (hidden.astype(F32) * gates).astype(BF)
    slope = up_pre * sig * (1.0 + gate_pre * (1.0 - sig))
    grad_hidden = dot(weight_down, routed, ((1,), (0,)))
    partial_gate = jnp.sum(hidden.astype(F32) * grad_hidden, axis=0, keepdims=True)
    d_act = gates * grad_hidden
    grad_gate = (d_act * slope).astype(BF)
    grad_up = (d_act * act).astype(BF)
    grads = jnp.concatenate([grad_gate, grad_up], 0)
    half = slots // 2
    share_a, _ = scatter_two_axes(both, grads[:, :half], "yz")
    share_b, seen = scatter_two_axes(both, grads[:, half:], "zy")
    share = jnp.concatenate([share_a, share_b], 1).astype(BF)
    slot_gate = sum_all(partial_gate)
    d_w_down = dot(fence(hidden_gated, seen[1])[0], routed, ((1,), (1,)), BF)
    d_w_gate = dot(inputs, fence(grad_gate, seen[2])[0], ((1,), (1,)), BF)
    d_w_up = dot(inputs, fence(grad_up, seen[3])[0], ((1,), (1,)), BF)

    send = jnp.concatenate([share] + three_parts(slot_gate) + [jnp.zeros((13, slots), BF)], 0)
    send = send.reshape(feats + 16, experts, most).transpose(1, 0, 2)
    back = lax.all_to_all(send, ("x", "c"), split_axis=0, concat_axis=0, tiled=True)
    back = back.transpose(1, 0, 2).reshape(feats + 16, slots)
    d_tokens = dot(chosen, back[:feats], ((1,), (1,)), BF)
    gate_back = jnp.sum(back[feats : feats + 3].astype(F32), axis=0)[None]
    lanes = jnp.arange(slots, dtype=jnp.int32)[None, :]
    zero = jnp.zeros((), F32)
    d_gates = jnp.stack(
        [jnp.sum(jnp.where(place[:, k : k + 1] == lanes, gate_back, zero), axis=1) for k in (0, 1)],
        axis=1,
    )
    return (d_tokens, d_gates, d_w_gate[None], d_w_up[None], d_w_down[None])


def solution(mesh):
    ep, et = mesh.axis_names
    nep, net = mesh.shape[ep], mesh.shape[et]
    fine = Mesh(mesh.devices.reshape(nep // 2, 2, net // 4, 4), ("x", "c", "z", "y"))
    e, t = ("x", "c"), ("z", "y")
    return jax.shard_map(
        shards,
        mesh=fine,
        in_specs=(P(e, t), P(e, None), P(e, None), P(e, t), P(e, None, t), P(e, None, t), P(e, t, None)),
        out_specs=(P(e, t), P(e, None), P(e, None, t), P(e, None, t), P(e, t, None)),
        check_vma=False,
    )
```

```python
import jax
import jax.numpy as jnp
from jax import lax
from jax.sharding import Mesh, PartitionSpec as P

BF = jnp.bfloat16
F32 = jnp.float32


def dot(left, right, dims, out=F32):
    return lax.dot_general(left, right, (dims, ((), ())), preferred_element_type=out)


def move(v, axis, step):
    n = lax.axis_size(axis)
    return lax.ppermute(v, axis, [(i, (i + step) % n) for i in range(n)])


def at(v, index, dim):
    return lax.dynamic_index_in_dim(v, index, dim, keepdims=False)


def put(buf, v, index, dim):
    return lax.dynamic_update_index_in_dim(buf, v, index, dim)


def ring_gather(v, axis, place, split):
    n = lax.axis_size(axis)
    me = lax.axis_index(axis)
    far = n // 2
    place(v, me, None)
    right = left = v
    for k in range(1, far):
        right = move(right, axis, 1)
        left = move(left, axis, -1)
        place(right, (me - k) % n, None)
        place(left, (me + k) % n, None)
    if split:
        half = v.shape[0] // 2
        place(move(right[:half], axis, 1), (me + far) % n, 0)
        place(move(left[half:], axis, -1), (me + far) % n, 1)
    else:
        place(move(right, axis, 1), (me + far) % n, None)


def gather_two_axes(x, order):
    rows, n = x.shape
    nz, ny = lax.axis_size("z"), lax.axis_size("y")
    size = lax.axis_size(order[0])
    part_of = [jnp.zeros((size, rows, n), x.dtype)]
    full = [jnp.zeros((nz, ny, rows, n), x.dtype)]

    def place_first(piece, owner, part):
        part_of[0] = put(part_of[0], piece, owner, 0)

    def place_second(piece, owner, part):
        low = 0 if part in (None, 0) else size // 2
        if order[0] == "z":
            full[0] = lax.dynamic_update_slice(full[0], piece[:, None], (low, owner, 0, 0))
        else:
            full[0] = lax.dynamic_update_slice(full[0], piece[None], (owner, low, 0, 0))

    ring_gather(x, order[0], place_first, False)
    ring_gather(part_of[0], order[1], place_second, True)
    return full[0].reshape(nz * ny * rows, n)


def ring_scatter(take, axis, split):
    n = lax.axis_size(axis)
    me = lax.axis_index(axis)
    far = n // 2
    left = None
    wait = None
    if split:
        right = move(take((me + far) % n, 0).astype(BF), axis, 1)
        seen = [right]
        right = right.astype(F32)
        left = move(take((me + far) % n, 1).astype(BF), axis, -1).astype(F32)
        pad = jnp.zeros_like(right)
        right = jnp.concatenate([right, pad], 0)
        left = jnp.concatenate([pad, left], 0)
    else:
        right = move(take((me + far) % n, None).astype(BF), axis, 1)
        seen = [right]
        right = right.astype(F32)
    for k in range(far - 1, 0, -1):
        right = move((take((me + k) % n, None, seen[0]) + right).astype(BF), axis, 1)
        seen.append(right)
        right = right.astype(F32)
        out = take((me - k) % n, None, seen[0])
        out = out if left is None else out + left
        left = move(out.astype(BF), axis, -1).astype(F32)
    return take(me, None, seen[0]) + right + left, seen


def halved(v, part):
    half = v.shape[0] // 2
    return v if part is None else v[:half] if part == 0 else v[half:]


def scatter_two_axes(weights, grads, order):
    nz, ny, rows, k = weights.shape
    n = grads.shape[1]

    def take_first(owner, part, arrived=None):
        after = grads if arrived is None else fence(grads, arrived)[0]
        own = halved(at(weights, owner, "zy".index(order[0])), part)
        return dot(own.reshape(-1, k), after, ((1,), (0,))).reshape(-1, rows, n)

    total, seen = ring_scatter(take_first, order[0], True)
    return ring_scatter(lambda owner, part, arrived=None: at(total, owner, 0), order[1], False)[0], seen


def fence(*values):
    return lax.optimization_barrier(values)


def three_parts(v):
    rows = []
    for _ in range(3):
        part = lax.reduce_precision(v, 8, 7)
        rows.append(part.astype(BF))
        v = v - part
    return rows


def sum_all(v):
    size = lax.axis_size("z") * lax.axis_size("y")
    rows = jnp.broadcast_to(v, (size, v.shape[1]))
    rows = lax.all_to_all(rows, ("z", "y"), split_axis=0, concat_axis=0, tiled=True)
    return jnp.sum(rows, axis=0, keepdims=True)


def shards(d_out, gate_weights, expert_ids, saved_inputs, w_gate, w_up, w_down):
    experts = lax.axis_size("x") * lax.axis_size("c")
    tok_rows, feats = d_out.shape
    most = tok_rows // 2
    slots = experts * most
    weight_gate, weight_up, weight_down = w_gate[0], w_up[0], w_down[0]

    flat = expert_ids.reshape(-1)
    onehot = (flat[:, None] == jnp.arange(experts, dtype=jnp.int32)[None, :]).astype(jnp.int32)
    before = jnp.cumsum(onehot, axis=0) - onehot
    place = (flat * most + jnp.sum(before * onehot, axis=1)).reshape(tok_rows, 2)
    lanes = jnp.arange(slots, dtype=jnp.int32)[None, :]
    hit0 = place[:, 0:1] == lanes
    hit1 = place[:, 1:2] == lanes
    chosen = (hit0 | hit1).astype(BF)
    zero = jnp.zeros((), F32)
    gates_out = jnp.sum(
        jnp.where(hit0, gate_weights[:, 0:1].astype(F32), zero)
        + jnp.where(hit1, gate_weights[:, 1:2].astype(F32), zero),
        axis=0,
    ).astype(BF)
    outgoing = dot(d_out, chosen, ((0,), (0,)), BF)
    extra = jnp.concatenate([gates_out[None], jnp.zeros((15, slots), BF)], 0)
    outgoing = jnp.concatenate([outgoing, extra], 0).reshape(feats + 16, experts, most)
    arrived = lax.all_to_all(
        outgoing.transpose(1, 0, 2), ("x", "c"), split_axis=0, concat_axis=0, tiled=True
    )
    arrived = arrived.transpose(1, 0, 2).reshape(feats + 16, slots)
    gates = arrived[feats : feats + 1].astype(F32)

    inputs = gather_two_axes(saved_inputs.T, "zy")
    routed = gather_two_axes(arrived[:feats], "yz")

    both = jnp.concatenate([weight_gate, weight_up], 1)
    both = both.reshape(lax.axis_size("z"), lax.axis_size("y"), feats, -1)
    gate_pre = dot(weight_gate, inputs, ((0,), (0,)))
    up_pre = dot(weight_up, inputs, ((0,), (0,)))
    sig = jax.nn.sigmoid(gate_pre)
    act = gate_pre * sig
    hidden = (act * up_pre).astype(BF)
    hidden_gated = (hidden.astype(F32) * gates).astype(BF)
    slope = up_pre * sig * (1.0 + gate_pre * (1.0 - sig))
    grad_hidden = dot(weight_down, routed, ((1,), (0,)))
    partial_gate = jnp.sum(hidden.astype(F32) * grad_hidden, axis=0, keepdims=True)
    d_act = gates * grad_hidden
    grad_gate = (d_act * slope).astype(BF)
    grad_up = (d_act * act).astype(BF)
    grads = jnp.concatenate([grad_gate, grad_up], 0)
    half = slots // 2
    share_a, _ = scatter_two_axes(both, grads[:, :half], "yz")
    share_b, seen = scatter_two_axes(both, grads[:, half:], "zy")
    share = jnp.concatenate([share_a, share_b], 1).astype(BF)
    slot_gate = sum_all(fence(partial_gate, seen[1])[0])
    d_w_down = dot(fence(hidden_gated, seen[1])[0], routed, ((1,), (1,)), BF)
    d_w_gate = dot(inputs, fence(grad_gate, seen[2])[0], ((1,), (1,)), BF)
    d_w_up = dot(inputs, fence(grad_up, seen[3])[0], ((1,), (1,)), BF)

    send = jnp.concatenate([share] + three_parts(slot_gate) + [jnp.zeros((13, slots), BF)], 0)
    send = send.reshape(feats + 16, experts, most).transpose(1, 0, 2)
    back = lax.all_to_all(send, ("x", "c"), split_axis=0, concat_axis=0, tiled=True)
    back = back.transpose(1, 0, 2).reshape(feats + 16, slots)
    d_tokens = dot(chosen, back[:feats], ((1,), (1,)), BF)
    gate_back = jnp.sum(back[feats : feats + 3].astype(F32), axis=0)[None]
    lanes = jnp.arange(slots, dtype=jnp.int32)[None, :]
    zero = jnp.zeros((), F32)
    d_gates = jnp.stack(
        [jnp.sum(jnp.where(place[:, k : k + 1] == lanes, gate_back, zero), axis=1) for k in (0, 1)],
        axis=1,
    )
    return (d_tokens, d_gates, d_w_gate[None], d_w_up[None], d_w_down[None])


def solution(mesh):
    ep, et = mesh.axis_names
    nep, net = mesh.shape[ep], mesh.shape[et]
    fine = Mesh(mesh.devices.reshape(nep // 2, 2, net // 4, 4), ("x", "c", "z", "y"))
    e, t = ("x", "c"), ("z", "y")
    return jax.shard_map(
        shards,
        mesh=fine,
        in_specs=(P(e, t), P(e, None), P(e, None), P(e, t), P(e, None, t), P(e, None, t), P(e, t, None)),
        out_specs=(P(e, t), P(e, None), P(e, None, t), P(e, None, t), P(e, t, None)),
        check_vma=False,
    )
```
